32 devices in a mesh: lat: 8 (over z, core), lon: 4 (over y, x).
Axes of the slice: x: 2, y: 2, z: 4, core: 2. Of those that a mesh axis runs over, the one named last changes fastest.
Arguments:
- queries: bfloat16 [16, 256, 2048], P('lat', 'lon'), may hold values from -50 to 50
- keyval: bfloat16 [2, 16, 256, 2048], P(None, 'lat', 'lon'), may hold values from -5 to 5
- keep: int32 [16], replicated, may hold values from 0 to 1, as said below
- lists: int32 [16, 8, 13], P('lat', 'lon'), may hold values from 0 to 14, as said below
Outputs:
- attended: bfloat16 [16, 256, 2048], P('lat', 'lon')
- gram_factor: float32 [8, 16, 128, 128], P('lat')
The draws below stay inside these ranges and needn't reach their ends.
Inputs may be any that keep to these rules, and one draw needn't show every extreme that they name: `lists`: each list holds 13 different candidate numbers; its first is 7, the query block itself. keep is 0 in rows 0 and 15, and 1 outside the first and last 4 rows.
All inputs are finite; a program needn't handle non-finite values.
Results may differ from the reference program's by a relative error of at most 0.015.
Values may be sent and summed in bfloat16 or wider, within the bound.
A program may use at most 64 MiB of HBM per device.

```python
import jax
import jax.numpy as jnp
from jax import lax

HEADS = 16
HD = 128
BLOCK = 32
HALO = 2
NB = 13
TLAT = 2
CAND = 15
NLAT = 16
NLON = 256
NBLK = 8
POLAR = 4
N_LAT = 8


def field_shape():
    return (NLAT, NLON, HEADS * HD)


def unit_normal(key, shape):
    return jnp.clip(jax.random.normal(key, shape, jnp.float32), -5.0, 5.0)


def draw_queries(key, part):
    return unit_normal(jax.random.fold_in(key, 3), field_shape()).astype(jnp.bfloat16)


def draw_keyval(key, part):
    keys_f = unit_normal(jax.random.fold_in(key, 1), field_shape())
    values_f = unit_normal(jax.random.fold_in(key, 2), field_shape())
    return jnp.stack([keys_f, values_f], 0).astype(jnp.bfloat16)


def draw_keep(key, part):
    row_index = jnp.arange(NLAT)
    coin_flip = jax.random.randint(jax.random.fold_in(key, 21), (NLAT,), 0, 2)
    polar_cap = (row_index < POLAR) | (row_index >= NLAT - POLAR)
    pole_rows = (row_index == 0) | (row_index == NLAT - 1)
    return jnp.where(pole_rows, 0, jnp.where(polar_cap, coin_flip, 1)).astype(jnp.int32)


def draw_lists(key, part):
    list_count = NLAT * NBLK
    raw_scores = jax.random.randint(jax.random.fold_in(key, 31), (list_count, CAND - 1), 0, 1 << 20) * 16
    raw_scores = raw_scores + jnp.arange(CAND - 1, dtype=jnp.int32)[None, :]
    ordering = jnp.argsort(raw_scores, axis=1).astype(jnp.int32)
    own_block = 3 * HALO + 1
    others = ordering[:, :NB - 1]
    others = others + (others >= own_block).astype(jnp.int32)
    complete = jnp.concatenate([jnp.full((list_count, 1), own_block, jnp.int32), others], axis=1)
    return complete.reshape(NLAT, NBLK, NB).astype(jnp.int32)


def setup_inputs(seed: int = 0) -> dict:
    splits = jax.random.split(jax.random.key(seed), 5)
    return {
        "queries": draw_queries(jax.random.fold_in(splits[4], 71), 0),
        "keyval": draw_keyval(jax.random.fold_in(splits[4], 71), 0),
        "keep": draw_keep(jax.random.fold_in(splits[4], 71), 0),
        "lists": draw_lists(jax.random.fold_in(splits[4], 71), 0),
    }


def row_attention(lat_row, queries, keyval, keep, lists):
    block_count = NLON // BLOCK
    query_row = lax.dynamic_index_in_dim(queries, lat_row, 0, keepdims=False)
    candidates = []
    usable_rows = []
    for offset in range(2 * HALO + 1):
        source = lat_row + offset - HALO
        clamped = jnp.clip(source, 0, NLAT - 1).astype(jnp.int32)
        row_slab = lax.dynamic_index_in_dim(keyval, clamped, 1, keepdims=False)
        row_slab = row_slab.reshape(2, block_count, BLOCK, HEADS * HD)
        for lon_step in range(3):
            candidates.append(jnp.roll(row_slab, 1 - lon_step, axis=1))
        inside = (source >= 0) & (source < NLAT)
        seen = jnp.logical_or(offset == HALO, lax.dynamic_index_in_dim(keep, clamped, 0, keepdims=False) == 1)
        usable_rows.append(inside & seen)
    stacked = jnp.moveaxis(jnp.stack(candidates, 0), 2, 0)
    row_lists = lax.dynamic_index_in_dim(lists, lat_row, 0, keepdims=False)
    chosen = jnp.take_along_axis(stacked, row_lists[:, :, None, None, None], axis=1)
    usable = jnp.stack(usable_rows, 0)[row_lists // 3]
    key_part = chosen[:, :, 0].reshape(block_count, NB * BLOCK, HEADS, HD).astype(jnp.float32)
    value_part = chosen[:, :, 1].reshape(block_count, NB * BLOCK, HEADS, HD).astype(jnp.float32)
    query_f32 = query_row.reshape(block_count, BLOCK, HEADS, HD).astype(jnp.float32)
    scores = jnp.einsum('bqhd,bkhd->bhqk', query_f32, key_part) * (HD ** -0.5)
    key_mask = jnp.repeat(usable, BLOCK, axis=1)[:, None, None, :]
    scores = jnp.where(key_mask, scores, -jnp.inf)
    row_top = jnp.max(scores, axis=-1, keepdims=True)
    weights = jnp.exp(scores - row_top)
    denominator = jnp.sum(weights, axis=-1)
    rounded = lax.optimization_barrier(weights.astype(jnp.bfloat16))
    mixture = jnp.einsum('bhqk,bkhd->bqhd', rounded.astype(jnp.float32), value_part)
    mixture = mixture / jnp.transpose(denominator, (0, 2, 1))[..., None]
    return mixture.reshape(NLON, HEADS * HD).astype(jnp.bfloat16)


def band_gram(band_rows):
    flat_rows = band_rows.astype(jnp.float32)
    return jnp.einsum('nhd,nhe->hde', flat_rows, flat_rows)


def reference(queries, keyval, keep, lists):
    attended = lax.map(lambda lat_row: row_attention(lat_row, queries, keyval, keep, lists), jnp.arange(NLAT, dtype=jnp.int32))
    bands = attended.reshape(N_LAT, TLAT * NLON, HEADS, HD)
    gram_factor = lax.map(band_gram, bands)
    return attended, gram_factor
```

```python
import functools
import math

import jax
import jax.numpy as jnp
from jax import lax
from jax.experimental import pallas as pl
from jax.experimental.pallas import tpu as pltpu
from jax.sharding import PartitionSpec as P

HEADS = 16
HD = 128
BLOCK = 32
HALO = 2
NB = 13
TLAT = 2
COLS = 64
GROUP = 2
NC = HEADS // GROUP
LANES = GROUP * HD
ROWS = TLAT + 2 * HALO
WIDE = COLS + 2 * BLOCK
KEYS = ROWS * WIDE
CELLS = TLAT * COLS
PACKED = HD + 16
AHEAD = 3
SCALE = HD ** (-0.5) * math.log2(math.e)
MESH = pl.DeviceIdType.MESH


def kernel(n_lat, n_lon, stages, q_hbm, kv_hbm, keep_ref, lists_ref, out_ref, gram_ref,
           ext, qs, bias, gsend, grecv,
           lon_send, lon_recv, own_send, own_recv, cor_send, cor_recv, gs_sem, gr_sem, loc_sem):
    lat = lax.axis_index("lat")
    lon = lax.axis_index("lon")
    west = lax.rem(lon + n_lon - 1, n_lon)
    east = lax.rem(lon + 1, n_lon)
    has_north = lat > 0
    has_south = lat < n_lat - 1
    partners = []
    for k in range(stages):
        bit = 1 << (stages - 1 - k)
        partners.append(lon + bit - 2 * bit * lax.rem(lon // bit, 2))

    barrier = pltpu.get_barrier_semaphore()
    for other in [west, east] + partners[:-1]:
        pl.semaphore_signal(barrier, inc=1, device_id=(lat, other), device_id_type=MESH)

    @pl.when(has_north)
    def _():
        pl.semaphore_signal(barrier, inc=1, device_id=(lat - 1, lon), device_id_type=MESH)

    @pl.when(has_south)
    def _():
        pl.semaphore_signal(barrier, inc=1, device_id=(lat + 1, lon), device_id_type=MESH)

    def lanes(c):
        return pl.ds(pl.multiple_of(c * LANES, LANES), LANES)

    def local_copies(c):
        return (
            pltpu.make_async_copy(
                kv_hbm.at[:, :, :, lanes(c)], ext.at[c, :, HALO : HALO + TLAT, 0:COLS], loc_sem.at[c, 0]
            ),
            pltpu.make_async_copy(q_hbm.at[:, :, lanes(c)], qs.at[c], loc_sem.at[c, 1]),
        )

    def local_start(c, carry):
        for copy in local_copies(c):
            copy.start()
        return carry

    lax.fori_loop(0, NC, local_start, 0)

    def remote(src, dst, send, recv, target):
        return pltpu.make_async_remote_copy(
            src_ref=src, dst_ref=dst, send_sem=send, recv_sem=recv, device_id=target, device_id_type=MESH
        )

    def to_west(c):
        return remote(
            kv_hbm.at[:, :, 0:BLOCK, lanes(c)],
            ext.at[c, :, HALO : HALO + TLAT, COLS + BLOCK : WIDE],
            lon_send.at[c, 0], lon_recv.at[c, 0], (lat, west),
        )

    def to_east(c):
        return remote(
            kv_hbm.at[:, :, COLS - BLOCK : COLS, lanes(c)],
            ext.at[c, :, HALO : HALO + TLAT, COLS : COLS + BLOCK],
            lon_send.at[c, 1], lon_recv.at[c, 1], (lat, east),
        )

    def own_north(c):
        return remote(
            kv_hbm.at[:, :, :, lanes(c)], ext.at[c, :, HALO + TLAT : ROWS, 0:COLS],
            own_send.at[c, 0], own_recv.at[c, 0], (lat - 1, lon),
        )

    def own_south(c):
        return remote(
            kv_hbm.at[:, :, :, lanes(c)], ext.at[c, :, 0:HALO, 0:COLS],
            own_send.at[c, 1], own_recv.at[c, 1], (lat + 1, lon),
        )

    def cor_north(c):
        return remote(
            ext.at[c, :, HALO : HALO + TLAT, COLS:WIDE], ext.at[c, :, HALO + TLAT : ROWS, COLS:WIDE],
            cor_send.at[c, 0], cor_recv.at[c, 0], (lat - 1, lon),
        )

    def cor_south(c):
        return remote(
            ext.at[c, :, HALO : HALO + TLAT, COLS:WIDE], ext.at[c, :, 0:HALO, COLS:WIDE],
            cor_send.at[c, 1], cor_recv.at[c, 1], (lat + 1, lon),
        )

    def gram_copy(k, c):
        return remote(
            gsend.at[k, c], grecv.at[k, c], gs_sem.at[k, c], gr_sem.at[k, c], (lat, partners[k])
        )

    def issue(c):
        to_west(c).start()
        to_east(c).start()

        @pl.when(has_north)
        def _():
            own_north(c).start()

        @pl.when(has_south)
        def _():
            own_south(c).start()

    pl.semaphore_wait(barrier, 1 + stages + has_north.astype(jnp.int32) + has_south.astype(jnp.int32))

    def first(c, carry):
        issue(c)
        return carry

    lax.fori_loop(0, min(AHEAD, NC), first, 0)

    @pl.when(jnp.logical_not(has_north))
    def _():
        def clear(c, carry):
            ext[c, :, 0:HALO] = jnp.zeros((2, HALO, WIDE, LANES), jnp.bfloat16)
            return carry
        lax.fori_loop(0, NC, clear, 0)

    @pl.when(jnp.logical_not(has_south))
    def _():
        def clear(c, carry):
            ext[c, :, HALO + TLAT : ROWS] = jnp.zeros((2, HALO, WIDE, LANES), jnp.bfloat16)
            return carry
        lax.fori_loop(0, NC, clear, 0)

    lane = lax.broadcasted_iota(jnp.int32, (8, KEYS), 1)
    row = lane // WIDE
    part = (lane - row * WIDE) // BLOCK
    total_rows = n_lat * TLAT
    kept = jnp.zeros((8, KEYS), jnp.int32)
    for e in range(ROWS):
        place = lat * TLAT - HALO + e
        flag = keep_ref[jnp.clip(place, 0, total_rows - 1)]
        kept = jnp.where(row == e, flag, kept)
    place = lat * TLAT - HALO + row
    inside = (place >= 0) & (place < total_rows)
    for t in range(TLAT):
        ok = inside & ((row == t + HALO) | (kept == 1)) & (row >= t) & (row <= t + 2 * HALO)
        for b in range(2):
            step = jnp.where(part == 0, 1 - b, jnp.where(part == 1, 2 - b, 0 if b == 0 else 2))
            ok_b = ok & (part != 3 - b)
            cand = 3 * (row - t) + step
            hit = cand == lists_ref[t, b, 0]
            for j in range(1, NB):
                hit = hit | (cand == lists_ref[t, b, j])
            value = jnp.where(ok_b & hit, 0.0, -jnp.inf).astype(jnp.float32)
            start = t * COLS + b * BLOCK
            for g in range(BLOCK // 8):
                bias[start + 8 * g : start + 8 * g + 8] = value

    ri = lax.broadcasted_iota(jnp.int32, (HD, HD), 0)
    ci = lax.broadcasted_iota(jnp.int32, (HD, HD), 1)

    def forward(c):
        to_west(c).wait_recv()
        to_east(c).wait_recv()

        @pl.when(has_north)
        def _():
            cor_north(c).start()

        @pl.when(has_south)
        def _():
            cor_south(c).start()

    def compute(c):
        for copy in local_copies(c):
            copy.wait()

        @pl.when(has_north)
        def _():
            own_south(c).wait_recv()
            cor_south(c).wait_recv()

        @pl.when(has_south)
        def _():
            own_north(c).wait_recv()
            cor_north(c).wait_recv()

        grams = []
        for g in range(GROUP):
            at = slice(g * HD, (g + 1) * HD)
            q = qs[c, :, :, at].reshape(CELLS, HD)
            k = ext[c, 0, :, :, at].reshape(KEYS, HD)
            v = ext[c, 1, :, :, at].reshape(KEYS, HD)
            s = lax.dot_general(q, k, (((1,), (1,)), ((), ())), preferred_element_type=jnp.float32)
            s = s + bias[...]
            top = jnp.max(s, axis=-1, keepdims=True)
            w = jnp.exp2((s - top) * SCALE)
            total = jnp.sum(w, axis=-1, keepdims=True)
            mix = jnp.dot(w.astype(jnp.bfloat16), v, preferred_element_type=jnp.float32)
            a = (mix / total).astype(jnp.bfloat16)
            out_ref[:, :, pl.ds(pl.multiple_of(c * LANES + g * HD, HD), HD)] = a.reshape(TLAT, COLS, HD)
            grams.append(
                lax.dot_general(a, a, (((0,), (0,)), ((), ())), preferred_element_type=jnp.float32)
            )
        g0, g1 = grams
        gsend[0, c, 0:HD] = jnp.where(ri <= ci, g0, g1).astype(jnp.bfloat16)
        diag = jnp.sum(jnp.where(ri == ci, g1, 0.0), axis=0, keepdims=True)
        gsend[0, c, HD:PACKED] = jnp.broadcast_to(diag, (PACKED - HD, HD)).astype(jnp.bfloat16)
        gram_copy(0, c).start()

    def gram_stage(k, c):
        gram_copy(k, c).wait_recv()
        both = gsend[k, c].astype(jnp.float32) + grecv[k, c].astype(jnp.float32)
        if k + 1 < stages:
            gsend[k + 1, c] = both.astype(jnp.bfloat16)
            gram_copy(k + 1, c).start()
        else:
            m = both[0:HD]
            mt = m.T
            d = jnp.broadcast_to(both[HD : HD + 1], (HD, HD))
            gram_ref[0, 2 * c] = jnp.where(ri <= ci, m, mt)
            gram_ref[0, 2 * c + 1] = jnp.where(ri > ci, m, jnp.where(ri == ci, d, mt))

    def step(s, carry):
        @pl.when(s + AHEAD < NC)
        def _():
            issue(s + AHEAD)

        @pl.when(s < NC)
        def _():
            forward(s)

        @pl.when((s >= 1) & (s <= NC))
        def _():
            compute(s - 1)

        for k in range(stages):
            @pl.when((s >= 2 + k) & (s < NC + 2 + k))
            def _():
                gram_stage(k, s - 2 - k)

        return carry

    lax.fori_loop(0, NC + 1 + stages, step, 0)

    def drain(c, carry):
        to_west(c).wait_send()
        to_east(c).wait_send()

        @pl.when(has_north)
        def _():
            own_north(c).wait_send()
            cor_north(c).wait_send()

        @pl.when(has_south)
        def _():
            own_south(c).wait_send()
            cor_south(c).wait_send()

        for k in range(stages):
            gram_copy(k, c).wait_send()
        return carry

    lax.fori_loop(0, NC, drain, 0)


def local(n_lat, n_lon, queries, keyval, keep, lists):
    stages = n_lon.bit_length() - 1
    assert n_lon == 1 << stages and queries.shape == (TLAT, COLS, HEADS * HD)
    dma = pltpu.SemaphoreType.DMA
    vmem = pl.BlockSpec(memory_space=pltpu.VMEM)
    smem = pl.BlockSpec(memory_space=pltpu.SMEM)
    hbm = pl.BlockSpec(memory_space=pl.ANY)
    return pl.pallas_call(
        functools.partial(kernel, n_lat, n_lon, stages),
        out_shape=(
            jax.ShapeDtypeStruct((TLAT, COLS, HEADS * HD), jnp.bfloat16),
            jax.ShapeDtypeStruct((1, HEADS, HD, HD), jnp.float32),
        ),
        in_specs=[hbm, hbm, smem, smem],
        out_specs=(vmem, vmem),
        scratch_shapes=[
            pltpu.VMEM((NC, 2, ROWS, WIDE, LANES), jnp.bfloat16),
            pltpu.VMEM((NC, TLAT, COLS, LANES), jnp.bfloat16),
            pltpu.VMEM((CELLS, KEYS), jnp.float32),
            pltpu.VMEM((stages, NC, PACKED, HD), jnp.bfloat16),
            pltpu.VMEM((stages, NC, PACKED, HD), jnp.bfloat16),
            dma((NC, 2)), dma((NC, 2)), dma((NC, 2)), dma((NC, 2)), dma((NC, 2)), dma((NC, 2)),
            dma((stages, NC)), dma((stages, NC)), dma((NC, 2)),
        ],
        compiler_params=pltpu.CompilerParams(
            collective_id=0, has_side_effects=True, vmem_limit_bytes=40 * 1024 * 1024
        ),
        cost_estimate=pl.CostEstimate(
            flops=4 * CELLS * KEYS * HEADS * HD, bytes_accessed=4 << 20, transcendentals=CELLS * KEYS * HEADS
        ),
    )(queries, keyval, keep, lists)


def solution(mesh):
    placed = (P("lat", "lon", None), P(None, "lat", "lon", None), P(), P("lat", "lon", None))
    return jax.shard_map(
        functools.partial(local, mesh.shape["lat"], mesh.shape["lon"]),
        mesh=mesh,
        in_specs=placed,
        out_specs=(P("lat", "lon", None), P("lat", None, None, None)),
        check_vma=False,
    )
```

```python
import functools
import math

import jax
import jax.numpy as jnp
from jax import lax
from jax.experimental import pallas as pl
from jax.experimental.pallas import tpu as pltpu
from jax.sharding import PartitionSpec as P

HEADS = 16
HD = 128
BLOCK = 32
HALO = 2
NB = 13
TLAT = 2
COLS = 64
GROUP = 2
NC = HEADS // GROUP
LANES = GROUP * HD
ROWS = TLAT + 2 * HALO
WIDE = COLS + 2 * BLOCK
KEYS = ROWS * WIDE
CELLS = TLAT * COLS
PACKED = HD + 16
SCALE = HD ** (-0.5) * math.log2(math.e)
MESH = pl.DeviceIdType.MESH


def kernel(n_lat, n_lon, stages, q_hbm, kv_hbm, keep_hbm, lists_hbm, out_ref, gram_ref,
           keep_ref, lists_ref, ext, qs, bias, gsend, grecv,
           lon_send, lon_recv, own_send, own_recv, cor_send, cor_recv, gs_sem, gr_sem, loc_sem, small_sem):
    lat = lax.axis_index("lat")
    lon = lax.axis_index("lon")
    west = lax.rem(lon + n_lon - 1, n_lon)
    east = lax.rem(lon + 1, n_lon)
    has_north = lat > 0
    has_south = lat < n_lat - 1
    partners = []
    for k in range(stages):
        bit = 1 << (stages - 1 - k)
        partners.append(lon + bit - 2 * bit * lax.rem(lon // bit, 2))

    barrier = pltpu.get_barrier_semaphore()
    for other in [west, east] + partners[:-1]:
        pl.semaphore_signal(barrier, inc=1, device_id=(lat, other), device_id_type=MESH)

    @pl.when(has_north)
    def _():
        pl.semaphore_signal(barrier, inc=1, device_id=(lat - 1, lon), device_id_type=MESH)

    @pl.when(has_south)
    def _():
        pl.semaphore_signal(barrier, inc=1, device_id=(lat + 1, lon), device_id_type=MESH)

    keep_copy = pltpu.make_async_copy(keep_hbm, keep_ref, small_sem.at[0])
    lists_copy = pltpu.make_async_copy(lists_hbm, lists_ref, small_sem.at[1])
    keep_copy.start()
    lists_copy.start()

    def lanes(c):
        return pl.ds(pl.multiple_of(c * LANES, LANES), LANES)

    def local_copies(c):
        return (
            pltpu.make_async_copy(
                kv_hbm.at[:, :, :, lanes(c)], ext.at[c, :, HALO : HALO + TLAT, 0:COLS], loc_sem.at[c, 0]
            ),
            pltpu.make_async_copy(q_hbm.at[:, :, lanes(c)], qs.at[c], loc_sem.at[c, 1]),
        )

    def local_start(c, carry):
        for copy in local_copies(c):
            copy.start()
        return carry

    lax.fori_loop(0, NC, local_start, 0)

    def remote(src, dst, send, recv, target):
        return pltpu.make_async_remote_copy(
            src_ref=src, dst_ref=dst, send_sem=send, recv_sem=recv, device_id=target, device_id_type=MESH
        )

    def to_west(c):
        return remote(
            kv_hbm.at[:, :, 0:BLOCK, lanes(c)],
            ext.at[c, :, HALO : HALO + TLAT, COLS + BLOCK : WIDE],
            lon_send.at[c, 0], lon_recv.at[c, 0], (lat, west),
        )

    def to_east(c):
        return remote(
            kv_hbm.at[:, :, COLS - BLOCK : COLS, lanes(c)],
            ext.at[c, :, HALO : HALO + TLAT, COLS : COLS + BLOCK],
            lon_send.at[c, 1], lon_recv.at[c, 1], (lat, east),
        )

    def own_north(c):
        return remote(
            kv_hbm.at[:, :, :, lanes(c)], ext.at[c, :, HALO + TLAT : ROWS, 0:COLS],
            own_send.at[c, 0], own_recv.at[c, 0], (lat - 1, lon),
        )

    def own_south(c):
        return remote(
            kv_hbm.at[:, :, :, lanes(c)], ext.at[c, :, 0:HALO, 0:COLS],
            own_send.at[c, 1], own_recv.at[c, 1], (lat + 1, lon),
        )

    def cor_north(c):
        return remote(
            ext.at[c, :, HALO : HALO + TLAT, COLS:WIDE], ext.at[c, :, HALO + TLAT : ROWS, COLS:WIDE],
            cor_send.at[c, 0], cor_recv.at[c, 0], (lat - 1, lon),
        )

    def cor_south(c):
        return remote(
            ext.at[c, :, HALO : HALO + TLAT, COLS:WIDE], ext.at[c, :, 0:HALO, COLS:WIDE],
            cor_send.at[c, 1], cor_recv.at[c, 1], (lat + 1, lon),
        )

    def gram_copy(k, c):
        return remote(
            gsend.at[k, c], grecv.at[k, c], gs_sem.at[k, c], gr_sem.at[k, c], (lat, partners[k])
        )

    def issue(c):
        to_west(c).start()
        to_east(c).start()

        @pl.when(has_north)
        def _():
            own_north(c).start()

        @pl.when(has_south)
        def _():
            own_south(c).start()

    pl.semaphore_wait(barrier, 1 + stages + has_north.astype(jnp.int32) + has_south.astype(jnp.int32))

    def first(c, carry):
        issue(c)
        return carry

    lax.fori_loop(0, NC, first, 0)

    @pl.when(jnp.logical_not(has_north))
    def _():
        def clear(c, carry):
            ext[c, :, 0:HALO] = jnp.zeros((2, HALO, WIDE, LANES), jnp.bfloat16)
            return carry
        lax.fori_loop(0, NC, clear, 0)

    @pl.when(jnp.logical_not(has_south))
    def _():
        def clear(c, carry):
            ext[c, :, HALO + TLAT : ROWS] = jnp.zeros((2, HALO, WIDE, LANES), jnp.bfloat16)
            return carry
        lax.fori_loop(0, NC, clear, 0)

    keep_copy.wait()
    lists_copy.wait()

    lane = lax.broadcasted_iota(jnp.int32, (8, KEYS), 1)
    row = lane // WIDE
    part = (lane - row * WIDE) // BLOCK
    total_rows = n_lat * TLAT
    kept = jnp.zeros((8, KEYS), jnp.int32)
    for e in range(ROWS):
        place = lat * TLAT - HALO + e
        flag = keep_ref[jnp.clip(place, 0, total_rows - 1)]
        kept = jnp.where(row == e, flag, kept)
    place = lat * TLAT - HALO + row
    inside = (place >= 0) & (place < total_rows)
    for t in range(TLAT):
        ok = inside & ((row == t + HALO) | (kept == 1)) & (row >= t) & (row <= t + 2 * HALO)
        for b in range(2):
            step = jnp.where(part == 0, 1 - b, jnp.where(part == 1, 2 - b, 0 if b == 0 else 2))
            ok_b = ok & (part != 3 - b)
            cand = 3 * (row - t) + step
            hit = cand == lists_ref[t, b, 0]
            for j in range(1, NB):
                hit = hit | (cand == lists_ref[t, b, j])
            value = jnp.where(ok_b & hit, 0.0, -jnp.inf).astype(jnp.float32)
            start = t * COLS + b * BLOCK
            for g in range(BLOCK // 8):
                bias[start + 8 * g : start + 8 * g + 8] = value

    ri = lax.broadcasted_iota(jnp.int32, (HD, HD), 0)
    ci = lax.broadcasted_iota(jnp.int32, (HD, HD), 1)

    def forward(c):
        to_west(c).wait_recv()
        to_east(c).wait_recv()

        @pl.when(has_north)
        def _():
            cor_north(c).start()

        @pl.when(has_south)
        def _():
            cor_south(c).start()

    def compute(c):
        for copy in local_copies(c):
            copy.wait()

        @pl.when(has_north)
        def _():
            own_south(c).wait_recv()
            cor_south(c).wait_recv()

        @pl.when(has_south)
        def _():
            own_north(c).wait_recv()
            cor_north(c).wait_recv()

        grams = []
        for g in range(GROUP):
            at = slice(g * HD, (g + 1) * HD)
            q = qs[c, :, :, at].reshape(CELLS, HD)
            k = ext[c, 0, :, :, at].reshape(KEYS, HD)
            v = ext[c, 1, :, :, at].reshape(KEYS, HD)
            s = lax.dot_general(q, k, (((1,), (1,)), ((), ())), preferred_element_type=jnp.float32)
            s = s + bias[...]
            top = jnp.max(s, axis=-1, keepdims=True)
            w = jnp.exp2((s - top) * SCALE)
            total = jnp.sum(w, axis=-1, keepdims=True)
            mix = jnp.dot(w.astype(jnp.bfloat16), v, preferred_element_type=jnp.float32)
            a = (mix / total).astype(jnp.bfloat16)
            out_ref[:, :, pl.ds(pl.multiple_of(c * LANES + g * HD, HD), HD)] = a.reshape(TLAT, COLS, HD)
            grams.append(
                lax.dot_general(a, a, (((0,), (0,)), ((), ())), preferred_element_type=jnp.float32)
            )
        g0, g1 = grams
        gsend[0, c, 0:HD] = jnp.where(ri <= ci, g0, g1).astype(jnp.bfloat16)
        diag = jnp.sum(jnp.where(ri == ci, g1, 0.0), axis=0, keepdims=True)
        gsend[0, c, HD:PACKED] = jnp.broadcast_to(diag, (PACKED - HD, HD)).astype(jnp.bfloat16)
        gram_copy(0, c).start()

    def gram_stage(k, c):
        gram_copy(k, c).wait_recv()
        both = gsend[k, c].astype(jnp.float32) + grecv[k, c].astype(jnp.float32)
        if k + 1 < stages:
            gsend[k + 1, c] = both.astype(jnp.bfloat16)
            gram_copy(k + 1, c).start()
        else:
            m = both[0:HD]
            mt = m.T
            d = jnp.broadcast_to(both[HD : HD + 1], (HD, HD))
            gram_ref[0, 2 * c] = jnp.where(ri <= ci, m, mt)
            gram_ref[0, 2 * c + 1] = jnp.where(ri > ci, m, jnp.where(ri == ci, d, mt))

    def step(s, carry):
        @pl.when(s < NC)
        def _():
            forward(s)

        @pl.when((s >= 1) & (s <= NC))
        def _():
            compute(s - 1)

        for k in range(stages):
            @pl.when((s >= 2 + k) & (s < NC + 2 + k))
            def _():
                gram_stage(k, s - 2 - k)

        return carry

    lax.fori_loop(0, NC + 1 + stages, step, 0)

    def drain(c, carry):
        to_west(c).wait_send()
        to_east(c).wait_send()

        @pl.when(has_north)
        def _():
            own_north(c).wait_send()
            cor_north(c).wait_send()

        @pl.when(has_south)
        def _():
            own_south(c).wait_send()
            cor_south(c).wait_send()

        for k in range(stages):
            gram_copy(k, c).wait_send()
        return carry

    lax.fori_loop(0, NC, drain, 0)


def local(n_lat, n_lon, queries, keyval, keep, lists):
    stages = n_lon.bit_length() - 1
    assert n_lon == 1 << stages and queries.shape == (TLAT, COLS, HEADS * HD)
    dma = pltpu.SemaphoreType.DMA
    vmem = pl.BlockSpec(memory_space=pltpu.VMEM)
    hbm = pl.BlockSpec(memory_space=pltpu.HBM)
    return pl.pallas_call(
        functools.partial(kernel, n_lat, n_lon, stages),
        out_shape=(
            jax.ShapeDtypeStruct((TLAT, COLS, HEADS * HD), jnp.bfloat16),
            jax.ShapeDtypeStruct((1, HEADS, HD, HD), jnp.float32),
        ),
        in_specs=[hbm] * 4,
        out_specs=(vmem, vmem),
        scratch_shapes=[
            pltpu.SMEM(keep.shape, jnp.int32),
            pltpu.SMEM(lists.shape, jnp.int32),
            pltpu.VMEM((NC, 2, ROWS, WIDE, LANES), jnp.bfloat16),
            pltpu.VMEM((NC, TLAT, COLS, LANES), jnp.bfloat16),
            pltpu.VMEM((CELLS, KEYS), jnp.float32),
            pltpu.VMEM((stages, NC, PACKED, HD), jnp.bfloat16),
            pltpu.VMEM((stages, NC, PACKED, HD), jnp.bfloat16),
            dma((NC, 2)), dma((NC, 2)), dma((NC, 2)), dma((NC, 2)), dma((NC, 2)), dma((NC, 2)),
            dma((stages, NC)), dma((stages, NC)), dma((NC, 2)), dma((2,)),
        ],
        compiler_params=pltpu.CompilerParams(
            collective_id=0, has_side_effects=True, vmem_limit_bytes=32 * 1024 * 1024
        ),
        cost_estimate=pl.CostEstimate(
            flops=4 * CELLS * KEYS * HEADS * HD, bytes_accessed=4 << 20, transcendentals=CELLS * KEYS * HEADS
        ),
    )(queries, keyval, keep, lists)


def solution(mesh):
    placed = (P("lat", "lon", None), P(None, "lat", "lon", None), P(), P("lat", "lon", None))
    return jax.shard_map(
        functools.partial(local, mesh.shape["lat"], mesh.shape["lon"]),
        mesh=mesh,
        in_specs=placed,
        out_specs=(P("lat", "lon", None), P("lat", None, None, None)),
        check_vma=False,
    )
```

```python
import functools
import math

import jax
import jax.numpy as jnp
from jax import lax
from jax.experimental import pallas as pl
from jax.experimental.pallas import tpu as pltpu
from jax.sharding import PartitionSpec as P

HEADS = 16
HD = 128
BLOCK = 32
HALO = 2
NB = 13
TLAT = 2
AHEAD = 2
COLS = 64
GROUP = 2
NC = HEADS // GROUP
LANES = GROUP * HD
ROWS = TLAT + 2 * HALO
WIDE = COLS + 2 * BLOCK
KEYS = ROWS * WIDE
CELLS = TLAT * COLS
PACKED = HD + 16
SCALE = HD ** (-0.5) * math.log2(math.e)
MESH = pl.DeviceIdType.MESH


def kernel(n_lat, n_lon, stages, q_hbm, kv_hbm, keep_hbm, lists_hbm, out_ref, gram_ref,
           keep_ref, lists_ref, ext, qs, bias, gsend, grecv,
           lon_send, lon_recv, own_send, own_recv, cor_send, cor_recv, gs_sem, gr_sem, loc_sem, small_sem):
    lat = lax.axis_index("lat")
    lon = lax.axis_index("lon")
    west = lax.rem(lon + n_lon - 1, n_lon)
    east = lax.rem(lon + 1, n_lon)
    has_north = lat > 0
    has_south = lat < n_lat - 1
    partners = []
    for k in range(stages):
        bit = 1 << (stages - 1 - k)
        partners.append(lon + bit - 2 * bit * lax.rem(lon // bit, 2))

    barrier = pltpu.get_barrier_semaphore()
    for other in [west, east] + partners[:-1]:
        pl.semaphore_signal(barrier, inc=1, device_id=(lat, other), device_id_type=MESH)

    @pl.when(has_north)
    def _():
        pl.semaphore_signal(barrier, inc=1, device_id=(lat - 1, lon), device_id_type=MESH)

    @pl.when(has_south)
    def _():
        pl.semaphore_signal(barrier, inc=1, device_id=(lat + 1, lon), device_id_type=MESH)

    keep_copy = pltpu.make_async_copy(keep_hbm, keep_ref, small_sem.at[0])
    lists_copy = pltpu.make_async_copy(lists_hbm, lists_ref, small_sem.at[1])
    keep_copy.start()
    lists_copy.start()

    def lanes(c):
        return pl.ds(pl.multiple_of(c * LANES, LANES), LANES)

    def local_copies(c):
        return (
            pltpu.make_async_copy(
                kv_hbm.at[:, :, :, lanes(c)], ext.at[c, :, HALO : HALO + TLAT, 0:COLS], loc_sem.at[c, 0]
            ),
            pltpu.make_async_copy(q_hbm.at[:, :, lanes(c)], qs.at[c], loc_sem.at[c, 1]),
        )

    def local_start(c, carry):
        for copy in local_copies(c):
            copy.start()
        return carry

    lax.fori_loop(0, NC, local_start, 0)

    def remote(src, dst, send, recv, target):
        return pltpu.make_async_remote_copy(
            src_ref=src, dst_ref=dst, send_sem=send, recv_sem=recv, device_id=target, device_id_type=MESH
        )

    def to_west(c):
        return remote(
            kv_hbm.at[:, :, 0:BLOCK, lanes(c)],
            ext.at[c, :, HALO : HALO + TLAT, COLS + BLOCK : WIDE],
            lon_send.at[c, 0], lon_recv.at[c, 0], (lat, west),
        )

    def to_east(c):
        return remote(
            kv_hbm.at[:, :, COLS - BLOCK : COLS, lanes(c)],
            ext.at[c, :, HALO : HALO + TLAT, COLS : COLS + BLOCK],
            lon_send.at[c, 1], lon_recv.at[c, 1], (lat, east),
        )

    def own_north(c):
        return remote(
            kv_hbm.at[:, :, :, lanes(c)], ext.at[c, :, HALO + TLAT : ROWS, 0:COLS],
            own_send.at[c, 0], own_recv.at[c, 0], (lat - 1, lon),
        )

    def own_south(c):
        return remote(
            kv_hbm.at[:, :, :, lanes(c)], ext.at[c, :, 0:HALO, 0:COLS],
            own_send.at[c, 1], own_recv.at[c, 1], (lat + 1, lon),
        )

    def cor_north(c):
        return remote(
            ext.at[c, :, HALO : HALO + TLAT, COLS:WIDE], ext.at[c, :, HALO + TLAT : ROWS, COLS:WIDE],
            cor_send.at[c, 0], cor_recv.at[c, 0], (lat - 1, lon),
        )

    def cor_south(c):
        return remote(
            ext.at[c, :, HALO : HALO + TLAT, COLS:WIDE], ext.at[c, :, 0:HALO, COLS:WIDE],
            cor_send.at[c, 1], cor_recv.at[c, 1], (lat + 1, lon),
        )

    def gram_copy(k, c):
        return remote(
            gsend.at[k, c], grecv.at[k, c], gs_sem.at[k, c], gr_sem.at[k, c], (lat, partners[k])
        )

    def issue(c):
        to_west(c).start()
        to_east(c).start()

        @pl.when(has_north)
        def _():
            own_north(c).start()

        @pl.when(has_south)
        def _():
            own_south(c).start()

    pl.semaphore_wait(barrier, 1 + stages + has_north.astype(jnp.int32) + has_south.astype(jnp.int32))

    def first(c, carry):
        issue(c)
        return carry

    lax.fori_loop(0, AHEAD, first, 0)

    @pl.when(jnp.logical_not(has_north))
    def _():
        def clear(c, carry):
            ext[c, :, 0:HALO] = jnp.zeros((2, HALO, WIDE, LANES), jnp.bfloat16)
            return carry
        lax.fori_loop(0, NC, clear, 0)

    @pl.when(jnp.logical_not(has_south))
    def _():
        def clear(c, carry):
            ext[c, :, HALO + TLAT : ROWS] = jnp.zeros((2, HALO, WIDE, LANES), jnp.bfloat16)
            return carry
        lax.fori_loop(0, NC, clear, 0)

    keep_copy.wait()
    lists_copy.wait()

    lane = lax.broadcasted_iota(jnp.int32, (8, KEYS), 1)
    row = lane // WIDE
    part = (lane - row * WIDE) // BLOCK
    total_rows = n_lat * TLAT
    kept = jnp.zeros((8, KEYS), jnp.int32)
    for e in range(ROWS):
        place = lat * TLAT - HALO + e
        flag = keep_ref[jnp.clip(place, 0, total_rows - 1)]
        kept = jnp.where(row == e, flag, kept)
    place = lat * TLAT - HALO + row
    inside = (place >= 0) & (place < total_rows)
    for t in range(TLAT):
        ok = inside & ((row == t + HALO) | (kept == 1)) & (row >= t) & (row <= t + 2 * HALO)
        for b in range(2):
            step = jnp.where(part == 0, 1 - b, jnp.where(part == 1, 2 - b, 0 if b == 0 else 2))
            ok_b = ok & (part != 3 - b)
            cand = 3 * (row - t) + step
            hit = cand == lists_ref[t, b, 0]
            for j in range(1, NB):
                hit = hit | (cand == lists_ref[t, b, j])
            value = jnp.where(ok_b & hit, 0.0, -jnp.inf).astype(jnp.float32)
            start = t * COLS + b * BLOCK
            for g in range(BLOCK // 8):
                bias[start + 8 * g : start + 8 * g + 8] = value

    ri = lax.broadcasted_iota(jnp.int32, (HD, HD), 0)
    ci = lax.broadcasted_iota(jnp.int32, (HD, HD), 1)

    def forward(c):
        to_west(c).wait_recv()
        to_east(c).wait_recv()

        @pl.when(has_north)
        def _():
            cor_north(c).start()

        @pl.when(has_south)
        def _():
            cor_south(c).start()

    def compute(c):
        for copy in local_copies(c):
            copy.wait()

        @pl.when(has_north)
        def _():
            own_south(c).wait_recv()
            cor_south(c).wait_recv()

        @pl.when(has_south)
        def _():
            own_north(c).wait_recv()
            cor_north(c).wait_recv()

        grams = []
        for g in range(GROUP):
            at = slice(g * HD, (g + 1) * HD)
            q = qs[c, :, :, at].reshape(CELLS, HD)
            k = ext[c, 0, :, :, at].reshape(KEYS, HD)
            v = ext[c, 1, :, :, at].reshape(KEYS, HD)
            s = lax.dot_general(q, k, (((1,), (1,)), ((), ())), preferred_element_type=jnp.float32)
            s = s + bias[...]
            top = jnp.max(s, axis=-1, keepdims=True)
            w = jnp.exp2((s - top) * SCALE)
            total = jnp.sum(w, axis=-1, keepdims=True)
            mix = jnp.dot(w.astype(jnp.bfloat16), v, preferred_element_type=jnp.float32)
            a = (mix / total).astype(jnp.bfloat16)
            out_ref[:, :, pl.ds(pl.multiple_of(c * LANES + g * HD, HD), HD)] = a.reshape(TLAT, COLS, HD)
            grams.append(
                lax.dot_general(a, a, (((0,), (0,)), ((), ())), preferred_element_type=jnp.float32)
            )
        g0, g1 = grams
        gsend[0, c, 0:HD] = jnp.where(ri <= ci, g0, g1).astype(jnp.bfloat16)
        diag = jnp.sum(jnp.where(ri == ci, g1, 0.0), axis=0, keepdims=True)
        gsend[0, c, HD:PACKED] = jnp.broadcast_to(diag, (PACKED - HD, HD)).astype(jnp.bfloat16)
        gram_copy(0, c).start()

    def gram_stage(k, c):
        gram_copy(k, c).wait_recv()
        both = gsend[k, c].astype(jnp.float32) + grecv[k, c].astype(jnp.float32)
        if k + 1 < stages:
            gsend[k + 1, c] = both.astype(jnp.bfloat16)
            gram_copy(k + 1, c).start()
        else:
            m = both[0:HD]
            mt = m.T
            d = jnp.broadcast_to(both[HD : HD + 1], (HD, HD))
            gram_ref[0, 2 * c] = jnp.where(ri <= ci, m, mt)
            gram_ref[0, 2 * c + 1] = jnp.where(ri > ci, m, jnp.where(ri == ci, d, mt))

    def step(s, carry):
        @pl.when(s < NC)
        def _():
            forward(s)

        @pl.when(s + AHEAD < NC)
        def _():
            issue(s + AHEAD)

        @pl.when((s >= 1) & (s <= NC))
        def _():
            compute(s - 1)

        for k in range(stages):
            @pl.when((s >= 2 + k) & (s < NC + 2 + k))
            def _():
                gram_stage(k, s - 2 - k)

        return carry

    lax.fori_loop(0, NC + 1 + stages, step, 0)

    def drain(c, carry):
        to_west(c).wait_send()
        to_east(c).wait_send()

        @pl.when(has_north)
        def _():
            own_north(c).wait_send()
            cor_north(c).wait_send()

        @pl.when(has_south)
        def _():
            own_south(c).wait_send()
            cor_south(c).wait_send()

        for k in range(stages):
            gram_copy(k, c).wait_send()
        return carry

    lax.fori_loop(0, NC, drain, 0)


def local(n_lat, n_lon, queries, keyval, keep, lists):
    stages = n_lon.bit_length() - 1
    assert n_lon == 1 << stages and queries.shape == (TLAT, COLS, HEADS * HD)
    dma = pltpu.SemaphoreType.DMA
    vmem = pl.BlockSpec(memory_space=pltpu.VMEM)
    hbm = pl.BlockSpec(memory_space=pltpu.HBM)
    return pl.pallas_call(
        functools.partial(kernel, n_lat, n_lon, stages),
        out_shape=(
            pltpu.VMEM((TLAT, COLS, HEADS * HD), jnp.bfloat16),
            pltpu.VMEM((1, HEADS, HD, HD), jnp.float32),
        ),
        in_specs=[hbm] * 4,
        out_specs=(vmem, vmem),
        scratch_shapes=[
            pltpu.SMEM(keep.shape, jnp.int32),
            pltpu.SMEM(lists.shape, jnp.int32),
            pltpu.VMEM((NC, 2, ROWS, WIDE, LANES), jnp.bfloat16),
            pltpu.VMEM((NC, TLAT, COLS, LANES), jnp.bfloat16),
            pltpu.VMEM((CELLS, KEYS), jnp.float32),
            pltpu.VMEM((stages, NC, PACKED, HD), jnp.bfloat16),
            pltpu.VMEM((stages, NC, PACKED, HD), jnp.bfloat16),
            dma((NC, 2)), dma((NC, 2)), dma((NC, 2)), dma((NC, 2)), dma((NC, 2)), dma((NC, 2)),
            dma((stages, NC)), dma((stages, NC)), dma((NC, 2)), dma((2,)),
        ],
        compiler_params=pltpu.CompilerParams(
            collective_id=0, has_side_effects=True, vmem_limit_bytes=32 * 1024 * 1024
        ),
        cost_estimate=pl.CostEstimate(
            flops=4 * CELLS * KEYS * HEADS * HD, bytes_accessed=4 << 20, transcendentals=CELLS * KEYS * HEADS
        ),
    )(*(pltpu.with_memory_space_constraint(x, pltpu.HBM) for x in (queries, keyval, keep, lists)))


def solution(mesh):
    placed = (P("lat", "lon", None), P(None, "lat", "lon", None), P(), P("lat", "lon", None))
    return jax.shard_map(
        functools.partial(local, mesh.shape["lat"], mesh.shape["lon"]),
        mesh=mesh,
        in_specs=placed,
        out_specs=(P("lat", "lon", None), P("lat", None, None, None)),
        check_vma=False,
    )
```

```python
import functools
import math

import jax
import jax.numpy as jnp
from jax import lax
from jax.experimental import pallas as pl
from jax.experimental.pallas import tpu as pltpu
from jax.sharding import PartitionSpec as P

HEADS = 16
HD = 128
BLOCK = 32
HALO = 2
NB = 13
TLAT = 2
AHEAD = 4
COLS = 64
GROUP = 2
NC = HEADS // GROUP
LANES = GROUP * HD
ROWS = TLAT + 2 * HALO
WIDE = COLS + 2 * BLOCK
KEYS = ROWS * WIDE
CELLS = TLAT * COLS
PACKED = HD + 16
SCALE = HD ** (-0.5) * math.log2(math.e)
MESH = pl.DeviceIdType.MESH


def kernel(n_lat, n_lon, stages, q_hbm, kv_hbm, keep_hbm, lists_hbm, out_ref, gram_ref,
           keep_ref, lists_ref, ext, qs, bias, gsend, grecv,
           lon_send, lon_recv, own_send, own_recv, cor_send, cor_recv, gs_sem, gr_sem, loc_sem, small_sem):
    lat = lax.axis_index("lat")
    lon = lax.axis_index("lon")
    west = lax.rem(lon + n_lon - 1, n_lon)
    east = lax.rem(lon + 1, n_lon)
    has_north = lat > 0
    has_south = lat < n_lat - 1
    partners = []
    for k in range(stages):
        bit = 1 << (stages - 1 - k)
        partners.append(lon + bit - 2 * bit * lax.rem(lon // bit, 2))

    barrier = pltpu.get_barrier_semaphore()
    for other in [west, east] + partners[:-1]:
        pl.semaphore_signal(barrier, inc=1, device_id=(lat, other), device_id_type=MESH)

    @pl.when(has_north)
    def _():
        pl.semaphore_signal(barrier, inc=1, device_id=(lat - 1, lon), device_id_type=MESH)

    @pl.when(has_south)
    def _():
        pl.semaphore_signal(barrier, inc=1, device_id=(lat + 1, lon), device_id_type=MESH)

    keep_copy = pltpu.make_async_copy(keep_hbm, keep_ref, small_sem.at[0])
    lists_copy = pltpu.make_async_copy(lists_hbm, lists_ref, small_sem.at[1])
    keep_copy.start()
    lists_copy.start()

    def lanes(c):
        return pl.ds(pl.multiple_of(c * LANES, LANES), LANES)

    def local_copies(c):
        return (
            pltpu.make_async_copy(
                kv_hbm.at[:, :, :, lanes(c)], ext.at[c, :, HALO : HALO + TLAT, 0:COLS], loc_sem.at[c, 0]
            ),
            pltpu.make_async_copy(q_hbm.at[:, :, lanes(c)], qs.at[c], loc_sem.at[c, 1]),
        )

    def local_start(c, carry):
        for copy in local_copies(c):
            copy.start()
        return carry

    lax.fori_loop(0, NC, local_start, 0)

    def remote(src, dst, send, recv, target):
        return pltpu.make_async_remote_copy(
            src_ref=src, dst_ref=dst, send_sem=send, recv_sem=recv, device_id=target, device_id_type=MESH
        )

    def to_west(c):
        return remote(
            kv_hbm.at[:, :, 0:BLOCK, lanes(c)],
            ext.at[c, :, HALO : HALO + TLAT, COLS + BLOCK : WIDE],
            lon_send.at[c, 0], lon_recv.at[c, 0], (lat, west),
        )

    def to_east(c):
        return remote(
            kv_hbm.at[:, :, COLS - BLOCK : COLS, lanes(c)],
            ext.at[c, :, HALO : HALO + TLAT, COLS : COLS + BLOCK],
            lon_send.at[c, 1], lon_recv.at[c, 1], (lat, east),
        )

    def own_north(c):
        return remote(
            kv_hbm.at[:, :, :, lanes(c)], ext.at[c, :, HALO + TLAT : ROWS, 0:COLS],
            own_send.at[c, 0], own_recv.at[c, 0], (lat - 1, lon),
        )

    def own_south(c):
        return remote(
            kv_hbm.at[:, :, :, lanes(c)], ext.at[c, :, 0:HALO, 0:COLS],
            own_send.at[c, 1], own_recv.at[c, 1], (lat + 1, lon),
        )

    def cor_north(c):
        return remote(
            ext.at[c, :, HALO : HALO + TLAT, COLS:WIDE], ext.at[c, :, HALO + TLAT : ROWS, COLS:WIDE],
            cor_send.at[c, 0], cor_recv.at[c, 0], (lat - 1, lon),
        )

    def cor_south(c):
        return remote(
            ext.at[c, :, HALO : HALO + TLAT, COLS:WIDE], ext.at[c, :, 0:HALO, COLS:WIDE],
            cor_send.at[c, 1], cor_recv.at[c, 1], (lat + 1, lon),
        )

    def gram_copy(k, c):
        return remote(
            gsend.at[k, c], grecv.at[k, c], gs_sem.at[k, c], gr_sem.at[k, c], (lat, partners[k])
        )

    def lon_issue(c):
        to_west(c).start()
        to_east(c).start()

    def own_issue(c):
        @pl.when(has_north)
        def _():
            own_north(c).start()

        @pl.when(has_south)
        def _():
            own_south(c).start()

    pl.semaphore_wait(barrier, 1 + stages + has_north.astype(jnp.int32) + has_south.astype(jnp.int32))

    def first(c, carry):
        lon_issue(c)
        return carry

    lax.fori_loop(0, AHEAD, first, 0)
    own_issue(0)

    @pl.when(jnp.logical_not(has_north))
    def _():
        def clear(c, carry):
            ext[c, :, 0:HALO] = jnp.zeros((2, HALO, WIDE, LANES), jnp.bfloat16)
            return carry
        lax.fori_loop(0, NC, clear, 0)

    @pl.when(jnp.logical_not(has_south))
    def _():
        def clear(c, carry):
            ext[c, :, HALO + TLAT : ROWS] = jnp.zeros((2, HALO, WIDE, LANES), jnp.bfloat16)
            return carry
        lax.fori_loop(0, NC, clear, 0)

    keep_copy.wait()
    lists_copy.wait()

    block = lax.broadcasted_iota(jnp.int32, (KEYS // BLOCK, CELLS), 0)
    lane = lax.broadcasted_iota(jnp.int32, (KEYS // BLOCK, CELLS), 1)
    row = block // (WIDE // BLOCK)
    part = block - row * (WIDE // BLOCK)
    t_of = lane // COLS
    b_of = (lane - t_of * COLS) // BLOCK
    total_rows = n_lat * TLAT
    kept = jnp.zeros_like(row)
    for e in range(ROWS):
        place = lat * TLAT - HALO + e
        flag = keep_ref[jnp.clip(place, 0, total_rows - 1)]
        kept = jnp.where(row == e, flag, kept)
    place = lat * TLAT - HALO + row
    ok = (place >= 0) & (place < total_rows) & ((row == t_of + HALO) | (kept == 1))
    ok = ok & (row >= t_of) & (row <= t_of + 2 * HALO) & (part != 3 - b_of)
    step_lon = jnp.where(part < 2, part + 1 - b_of, 2 * b_of)
    cand = 3 * (row - t_of) + step_lon
    hit = jnp.zeros_like(row)
    for t in range(TLAT):
        for b in range(2):
            here = cand == lists_ref[t, b, 0]
            for j in range(1, NB):
                here = here | (cand == lists_ref[t, b, j])
            hit = jnp.where(here & (t_of == t) & (b_of == b), 1, hit)
    value = jnp.where(ok & (hit == 1), 0.0, -jnp.inf).astype(jnp.float32)
    for n in range(KEYS // BLOCK):
        bias[n] = jnp.broadcast_to(value[n : n + 1], (8, CELLS))

    ri = lax.broadcasted_iota(jnp.int32, (HD, HD), 0)
    ci = lax.broadcasted_iota(jnp.int32, (HD, HD), 1)

    def forward(c):
        to_west(c).wait_recv()
        to_east(c).wait_recv()

        @pl.when(has_north)
        def _():
            cor_north(c).start()

        @pl.when(has_south)
        def _():
            cor_south(c).start()

    def compute(c):
        for copy in local_copies(c):
            copy.wait()

        @pl.when(has_north)
        def _():
            own_south(c).wait_recv()
            cor_south(c).wait_recv()

        @pl.when(has_south)
        def _():
            own_north(c).wait_recv()
            cor_north(c).wait_recv()

        grams = []
        for g in range(GROUP):
            at = slice(g * HD, (g + 1) * HD)
            q = qs[c, :, :, at].reshape(CELLS, HD)
            k = ext[c, 0, :, :, at].reshape(KEYS, HD)
            v = ext[c, 1, :, :, at].reshape(KEYS, HD)
            s = lax.dot_general(k, q, (((1,), (1,)), ((), ())), preferred_element_type=jnp.float32)
            s = s.reshape(KEYS // BLOCK, BLOCK // 8, 8, CELLS) + bias[...][:, None]
            top = jnp.max(jnp.max(s, axis=(0, 1)), axis=0, keepdims=True)
            w = jnp.exp2((s - top) * SCALE)
            total = jnp.sum(jnp.sum(w, axis=(0, 1)), axis=0, keepdims=True)
            w = w.reshape(KEYS, CELLS).astype(jnp.bfloat16)
            mix = lax.dot_general(v, w, (((0,), (0,)), ((), ())), preferred_element_type=jnp.float32)
            mix = mix * (1.0 / total)
            a = mix.astype(jnp.bfloat16)
            out_ref[:, :, pl.ds(pl.multiple_of(c * LANES + g * HD, HD), HD)] = (
                mix.T.astype(jnp.bfloat16).reshape(TLAT, COLS, HD)
            )
            grams.append(
                lax.dot_general(a, a, (((1,), (1,)), ((), ())), preferred_element_type=jnp.float32)
            )
        g0, g1 = grams
        gsend[0, c, 0:HD] = jnp.where(ri <= ci, g0, g1).astype(jnp.bfloat16)
        diag = jnp.sum(jnp.where(ri == ci, g1, 0.0), axis=0, keepdims=True)
        gsend[0, c, HD:PACKED] = jnp.broadcast_to(diag, (PACKED - HD, HD)).astype(jnp.bfloat16)
        gram_copy(0, c).start()

    def gram_stage(k, c):
        gram_copy(k, c).wait_recv()
        both = gsend[k, c].astype(jnp.float32) + grecv[k, c].astype(jnp.float32)
        if k + 1 < stages:
            gsend[k + 1, c] = both.astype(jnp.bfloat16)
            gram_copy(k + 1, c).start()
        else:
            m = both[0:HD]
            mt = m.T
            d = jnp.broadcast_to(both[HD : HD + 1], (HD, HD))
            gram_ref[0, 2 * c] = jnp.where(ri <= ci, m, mt)
            gram_ref[0, 2 * c + 1] = jnp.where(ri > ci, m, jnp.where(ri == ci, d, mt))

    def step(s, carry):
        @pl.when(s < NC)
        def _():
            forward(s)

        @pl.when(s + AHEAD < NC)
        def _():
            lon_issue(s + AHEAD)

        @pl.when(s + 1 < NC)
        def _():
            own_issue(s + 1)

        @pl.when((s >= 1) & (s <= NC))
        def _():
            compute(s - 1)

        for k in range(stages):
            @pl.when((s >= 2 + k) & (s < NC + 2 + k))
            def _():
                gram_stage(k, s - 2 - k)

        return carry

    lax.fori_loop(0, NC + 1 + stages, step, 0)

    def drain(c, carry):
        to_west(c).wait_send()
        to_east(c).wait_send()

        @pl.when(has_north)
        def _():
            own_north(c).wait_send()
            cor_north(c).wait_send()

        @pl.when(has_south)
        def _():
            own_south(c).wait_send()
            cor_south(c).wait_send()

        for k in range(stages):
            gram_copy(k, c).wait_send()
        return carry

    lax.fori_loop(0, NC, drain, 0)


def local(n_lat, n_lon, queries, keyval, keep, lists):
    stages = n_lon.bit_length() - 1
    assert n_lon == 1 << stages and queries.shape == (TLAT, COLS, HEADS * HD)
    dma = pltpu.SemaphoreType.DMA
    vmem = pl.BlockSpec(memory_space=pltpu.VMEM)
    hbm = pl.BlockSpec(memory_space=pltpu.HBM)
    return pl.pallas_call(
        functools.partial(kernel, n_lat, n_lon, stages),
        out_shape=(
            pltpu.VMEM((TLAT, COLS, HEADS * HD), jnp.bfloat16),
            pltpu.VMEM((1, HEADS, HD, HD), jnp.float32),
        ),
        in_specs=[hbm] * 4,
        out_specs=(vmem, vmem),
        scratch_shapes=[
            pltpu.SMEM(keep.shape, jnp.int32),
            pltpu.SMEM(lists.shape, jnp.int32),
            pltpu.VMEM((NC, 2, ROWS, WIDE, LANES), jnp.bfloat16),
            pltpu.VMEM((NC, TLAT, COLS, LANES), jnp.bfloat16),
            pltpu.VMEM((KEYS // BLOCK, 8, CELLS), jnp.float32),
            pltpu.VMEM((stages, NC, PACKED, HD), jnp.bfloat16),
            pltpu.VMEM((stages, NC, PACKED, HD), jnp.bfloat16),
            dma((NC, 2)), dma((NC, 2)), dma((NC, 2)), dma((NC, 2)), dma((NC, 2)), dma((NC, 2)),
            dma((stages, NC)), dma((stages, NC)), dma((NC, 2)), dma((2,)),
        ],
        compiler_params=pltpu.CompilerParams(
            collective_id=0, has_side_effects=True, vmem_limit_bytes=32 * 1024 * 1024
        ),
        cost_estimate=pl.CostEstimate(
            flops=4 * CELLS * KEYS * HEADS * HD, bytes_accessed=4 << 20, transcendentals=CELLS * KEYS * HEADS
        ),
    )(*(pltpu.with_memory_space_constraint(x, pltpu.HBM) for x in (queries, keyval, keep, lists)))


def solution(mesh):
    placed = (P("lat", "lon", None), P(None, "lat", "lon", None), P(), P("lat", "lon", None))
    return jax.shard_map(
        functools.partial(local, mesh.shape["lat"], mesh.shape["lon"]),
        mesh=mesh,
        in_specs=placed,
        out_specs=(P("lat", "lon", None), P("lat", None, None, None)),
        check_vma=False,
    )
```

```python
import functools
import math

import jax
import jax.numpy as jnp
from jax import lax
from jax.experimental import pallas as pl
from jax.experimental.pallas import tpu as pltpu
from jax.sharding import PartitionSpec as P

HEADS = 16
HD = 128
BLOCK = 32
HALO = 2
NB = 13
TLAT = 2
AHEAD = 2
COLS = 64
GROUP = 2
NC = HEADS // GROUP
LANES = GROUP * HD
ROWS = TLAT + 2 * HALO
WIDE = COLS + 2 * BLOCK
KEYS = ROWS * WIDE
CELLS = TLAT * COLS
PACKED = HD + 16
SCALE = HD ** (-0.5) * math.log2(math.e)
MESH = pl.DeviceIdType.MESH


def kernel(n_lat, n_lon, stages, q_hbm, kv_hbm, keep_hbm, lists_hbm, out_ref, gram_ref,
           keep_ref, lists_ref, ext, qs, bias, gsend, grecv,
           lon_send, lon_recv, own_send, own_recv, cor_send, cor_recv, gs_sem, gr_sem, loc_sem, small_sem):
    lat = lax.axis_index("lat")
    lon = lax.axis_index("lon")
    west = lax.rem(lon + n_lon - 1, n_lon)
    east = lax.rem(lon + 1, n_lon)
    has_north = lat > 0
    has_south = lat < n_lat - 1
    partners = []
    for k in range(stages):
        bit = 1 << (stages - 1 - k)
        partners.append(lon + bit - 2 * bit * lax.rem(lon // bit, 2))

    barrier = pltpu.get_barrier_semaphore()
    for other in [west, east] + partners[:-1]:
        pl.semaphore_signal(barrier, inc=1, device_id=(lat, other), device_id_type=MESH)

    @pl.when(has_north)
    def _():
        pl.semaphore_signal(barrier, inc=1, device_id=(lat - 1, lon), device_id_type=MESH)

    @pl.when(has_south)
    def _():
        pl.semaphore_signal(barrier, inc=1, device_id=(lat + 1, lon), device_id_type=MESH)

    keep_copy = pltpu.make_async_copy(keep_hbm, keep_ref, small_sem.at[0])
    lists_copy = pltpu.make_async_copy(lists_hbm, lists_ref, small_sem.at[1])
    keep_copy.start()
    lists_copy.start()

    def lanes(c):
        return pl.ds(pl.multiple_of(c * LANES, LANES), LANES)

    def local_copies(c):
        return (
            pltpu.make_async_copy(
                kv_hbm.at[:, :, :, lanes(c)], ext.at[c, :, HALO : HALO + TLAT, 0:COLS], loc_sem.at[c, 0]
            ),
            pltpu.make_async_copy(q_hbm.at[:, :, lanes(c)], qs.at[c], loc_sem.at[c, 1]),
        )

    def local_start(c, carry):
        for copy in local_copies(c):
            copy.start()
        return carry

    lax.fori_loop(0, NC, local_start, 0)

    def remote(src, dst, send, recv, target):
        return pltpu.make_async_remote_copy(
            src_ref=src, dst_ref=dst, send_sem=send, recv_sem=recv, device_id=target, device_id_type=MESH
        )

    def to_west(c):
        return remote(
            kv_hbm.at[:, :, 0:BLOCK, lanes(c)],
            ext.at[c, :, HALO : HALO + TLAT, COLS + BLOCK : WIDE],
            lon_send.at[c, 0], lon_recv.at[c, 0], (lat, west),
        )

    def to_east(c):
        return remote(
            kv_hbm.at[:, :, COLS - BLOCK : COLS, lanes(c)],
            ext.at[c, :, HALO : HALO + TLAT, COLS : COLS + BLOCK],
            lon_send.at[c, 1], lon_recv.at[c, 1], (lat, east),
        )

    def own_north(c):
        return remote(
            kv_hbm.at[:, :, :, lanes(c)], ext.at[c, :, HALO + TLAT : ROWS, 0:COLS],
            own_send.at[c, 0], own_recv.at[c, 0], (lat - 1, lon),
        )

    def own_south(c):
        return remote(
            kv_hbm.at[:, :, :, lanes(c)], ext.at[c, :, 0:HALO, 0:COLS],
            own_send.at[c, 1], own_recv.at[c, 1], (lat + 1, lon),
        )

    def cor_north(c):
        return remote(
            ext.at[c, :, HALO : HALO + TLAT, COLS:WIDE], ext.at[c, :, HALO + TLAT : ROWS, COLS:WIDE],
            cor_send.at[c, 0], cor_recv.at[c, 0], (lat - 1, lon),
        )

    def cor_south(c):
        return remote(
            ext.at[c, :, HALO : HALO + TLAT, COLS:WIDE], ext.at[c, :, 0:HALO, COLS:WIDE],
            cor_send.at[c, 1], cor_recv.at[c, 1], (lat + 1, lon),
        )

    def gram_copy(k, c):
        return remote(
            gsend.at[k, c], grecv.at[k, c], gs_sem.at[k, c], gr_sem.at[k, c], (lat, partners[k])
        )

    def lon_issue(c):
        to_west(c).start()
        to_east(c).start()

    def own_issue(c):
        @pl.when(has_north)
        def _():
            own_north(c).start()

        @pl.when(has_south)
        def _():
            own_south(c).start()

    pl.semaphore_wait(barrier, 1 + stages + has_north.astype(jnp.int32) + has_south.astype(jnp.int32))

    def first(c, carry):
        lon_issue(c)
        own_issue(c)
        return carry

    lax.fori_loop(0, AHEAD, first, 0)

    @pl.when(jnp.logical_not(has_north))
    def _():
        def clear(c, carry):
            ext[c, :, 0:HALO] = jnp.zeros((2, HALO, WIDE, LANES), jnp.bfloat16)
            return carry
        lax.fori_loop(0, NC, clear, 0)

    @pl.when(jnp.logical_not(has_south))
    def _():
        def clear(c, carry):
            ext[c, :, HALO + TLAT : ROWS] = jnp.zeros((2, HALO, WIDE, LANES), jnp.bfloat16)
            return carry
        lax.fori_loop(0, NC, clear, 0)

    keep_copy.wait()
    lists_copy.wait()

    block = lax.broadcasted_iota(jnp.int32, (KEYS // BLOCK, CELLS), 0)
    lane = lax.broadcasted_iota(jnp.int32, (KEYS // BLOCK, CELLS), 1)
    row = block // (WIDE // BLOCK)
    part = block - row * (WIDE // BLOCK)
    t_of = lane // COLS
    b_of = (lane - t_of * COLS) // BLOCK
    total_rows = n_lat * TLAT
    kept = jnp.zeros_like(row)
    for e in range(ROWS):
        place = lat * TLAT - HALO + e
        flag = keep_ref[jnp.clip(place, 0, total_rows - 1)]
        kept = jnp.where(row == e, flag, kept)
    place = lat * TLAT - HALO + row
    ok = (place >= 0) & (place < total_rows) & ((row == t_of + HALO) | (kept == 1))
    ok = ok & (row >= t_of) & (row <= t_of + 2 * HALO) & (part != 3 - b_of)
    step_lon = jnp.where(part < 2, part + 1 - b_of, 2 * b_of)
    cand = 3 * (row - t_of) + step_lon
    hit = jnp.zeros_like(row)
    for t in range(TLAT):
        for b in range(2):
            here = cand == lists_ref[t, b, 0]
            for j in range(1, NB):
                here = here | (cand == lists_ref[t, b, j])
            hit = jnp.where(here & (t_of == t) & (b_of == b), 1, hit)
    value = jnp.where(ok & (hit == 1), 0.0, -jnp.inf).astype(jnp.float32)
    for n in range(KEYS // BLOCK):
        bias[n] = jnp.broadcast_to(value[n : n + 1], (8, CELLS))

    ri = lax.broadcasted_iota(jnp.int32, (HD, HD), 0)
    ci = lax.broadcasted_iota(jnp.int32, (HD, HD), 1)

    def forward(c):
        to_west(c).wait_recv()
        to_east(c).wait_recv()

        @pl.when(has_north)
        def _():
            cor_north(c).start()

        @pl.when(has_south)
        def _():
            cor_south(c).start()

    def compute(c):
        for copy in local_copies(c):
            copy.wait()

        @pl.when(has_north)
        def _():
            own_south(c).wait_recv()
            cor_south(c).wait_recv()

        @pl.when(has_south)
        def _():
            own_north(c).wait_recv()
            cor_north(c).wait_recv()

        grams = []
        for g in range(GROUP):
            at = slice(g * HD, (g + 1) * HD)
            q = qs[c, :, :, at].reshape(CELLS, HD)
            k = ext[c, 0, :, :, at].reshape(KEYS, HD)
            v = ext[c, 1, :, :, at].reshape(KEYS, HD)
            s = lax.dot_general(k, q, (((1,), (1,)), ((), ())), preferred_element_type=jnp.float32)
            s = s.reshape(KEYS // BLOCK, BLOCK // 8, 8, CELLS) + bias[...][:, None]
            top = jnp.max(jnp.max(s, axis=(0, 1)), axis=0, keepdims=True)
            w = jnp.exp2((s - top) * SCALE)
            total = jnp.sum(jnp.sum(w, axis=(0, 1)), axis=0, keepdims=True)
            w = w.reshape(KEYS, CELLS).astype(jnp.bfloat16)
            mix = lax.dot_general(v, w, (((0,), (0,)), ((), ())), preferred_element_type=jnp.float32)
            mix = mix * (1.0 / total)
            a = mix.astype(jnp.bfloat16)
            out_ref[:, :, pl.ds(pl.multiple_of(c * LANES + g * HD, HD), HD)] = (
                mix.T.astype(jnp.bfloat16).reshape(TLAT, COLS, HD)
            )
            grams.append(
                lax.dot_general(a, a, (((1,), (1,)), ((), ())), preferred_element_type=jnp.float32)
            )
        g0, g1 = grams
        gsend[0, c, 0:HD] = jnp.where(ri <= ci, g0, g1).astype(jnp.bfloat16)
        diag = jnp.sum(jnp.where(ri == ci, g1, 0.0), axis=0, keepdims=True)
        gsend[0, c, HD:PACKED] = jnp.broadcast_to(diag, (PACKED - HD, HD)).astype(jnp.bfloat16)
        gram_copy(0, c).start()

    def gram_stage(k, c):
        gram_copy(k, c).wait_recv()
        both = gsend[k, c].astype(jnp.float32) + grecv[k, c].astype(jnp.float32)
        if k + 1 < stages:
            gsend[k + 1, c] = both.astype(jnp.bfloat16)
            gram_copy(k + 1, c).start()
        else:
            m = both[0:HD]
            mt = m.T
            d = jnp.broadcast_to(both[HD : HD + 1], (HD, HD))
            gram_ref[0, 2 * c] = jnp.where(ri <= ci, m, mt)
            gram_ref[0, 2 * c + 1] = jnp.where(ri > ci, m, jnp.where(ri == ci, d, mt))

    def step(s, carry):
        @pl.when(s < NC)
        def _():
            forward(s)

        @pl.when(s + AHEAD < NC)
        def _():
            lon_issue(s + AHEAD)
            own_issue(s + AHEAD)

        @pl.when((s >= 1) & (s <= NC))
        def _():
            compute(s - 1)

        for k in range(stages):
            @pl.when((s >= 2 + k) & (s < NC + 2 + k))
            def _():
                gram_stage(k, s - 2 - k)

        return carry

    lax.fori_loop(0, NC + 1 + stages, step, 0)

    def drain(c, carry):
        to_west(c).wait_send()
        to_east(c).wait_send()

        @pl.when(has_north)
        def _():
            own_north(c).wait_send()
            cor_north(c).wait_send()

        @pl.when(has_south)
        def _():
            own_south(c).wait_send()
            cor_south(c).wait_send()

        for k in range(stages):
            gram_copy(k, c).wait_send()
        return carry

    lax.fori_loop(0, NC, drain, 0)


def local(n_lat, n_lon, queries, keyval, keep, lists):
    stages = n_lon.bit_length() - 1
    assert n_lon == 1 << stages and queries.shape == (TLAT, COLS, HEADS * HD)
    dma = pltpu.SemaphoreType.DMA
    vmem = pl.BlockSpec(memory_space=pltpu.VMEM)
    hbm = pl.BlockSpec(memory_space=pltpu.HBM)
    return pl.pallas_call(
        functools.partial(kernel, n_lat, n_lon, stages),
        out_shape=(
            pltpu.VMEM((TLAT, COLS, HEADS * HD), jnp.bfloat16),
            pltpu.VMEM((1, HEADS, HD, HD), jnp.float32),
        ),
        in_specs=[hbm] * 4,
        out_specs=(vmem, vmem),
        scratch_shapes=[
            pltpu.SMEM(keep.shape, jnp.int32),
            pltpu.SMEM(lists.shape, jnp.int32),
            pltpu.VMEM((NC, 2, ROWS, WIDE, LANES), jnp.bfloat16),
            pltpu.VMEM((NC, TLAT, COLS, LANES), jnp.bfloat16),
            pltpu.VMEM((KEYS // BLOCK, 8, CELLS), jnp.float32),
            pltpu.VMEM((stages, NC, PACKED, HD), jnp.bfloat16),
            pltpu.VMEM((stages, NC, PACKED, HD), jnp.bfloat16),
            dma((NC, 2)), dma((NC, 2)), dma((NC, 2)), dma((NC, 2)), dma((NC, 2)), dma((NC, 2)),
            dma((stages, NC)), dma((stages, NC)), dma((NC, 2)), dma((2,)),
        ],
        compiler_params=pltpu.CompilerParams(
            collective_id=0, has_side_effects=True, vmem_limit_bytes=32 * 1024 * 1024
        ),
        cost_estimate=pl.CostEstimate(
            flops=4 * CELLS * KEYS * HEADS * HD, bytes_accessed=4 << 20, transcendentals=CELLS * KEYS * HEADS
        ),
    )(*(pltpu.with_memory_space_constraint(x, pltpu.HBM) for x in (queries, keyval, keep, lists)))


def solution(mesh):
    placed = (P("lat", "lon", None), P(None, "lat", "lon", None), P(), P("lat", "lon", None))
    return jax.shard_map(
        functools.partial(local, mesh.shape["lat"], mesh.shape["lon"]),
        mesh=mesh,
        in_specs=placed,
        out_specs=(P("lat", "lon", None), P("lat", None, None, None)),
        check_vma=False,
    )
```

```python
import functools
import math

import jax
import jax.numpy as jnp
from jax import lax
from jax.experimental import pallas as pl
from jax.experimental.pallas import tpu as pltpu
from jax.sharding import PartitionSpec as P

HEADS = 16
HD = 128
BLOCK = 32
HALO = 2
NB = 13
TLAT = 2
AHEAD = 2
COLS = 64
GROUP = 2
NC = HEADS // GROUP
LANES = GROUP * HD
ROWS = TLAT + 2 * HALO
WIDE = COLS + 2 * BLOCK
KEYS = ROWS * WIDE
CELLS = TLAT * COLS
PACKED = HD + 16
SCALE = HD ** (-0.5) * math.log2(math.e)
MESH = pl.DeviceIdType.MESH


def kernel(n_lat, n_lon, stages, q_hbm, kv_hbm, keep_hbm, lists_hbm, out_ref, gram_ref,
           keep_ref, lists_ref, ext, qs, bias, gsend, grecv,
           lon_send, lon_recv, own_send, own_recv, cor_send, cor_recv, gs_sem, gr_sem, loc_sem, small_sem):
    lat = lax.axis_index("lat")
    lon = lax.axis_index("lon")
    west = lax.rem(lon + n_lon - 1, n_lon)
    east = lax.rem(lon + 1, n_lon)
    has_north = lat > 0
    has_south = lat < n_lat - 1
    partners = []
    for k in range(stages):
        bit = 1 << (stages - 1 - k)
        partners.append(lon + bit - 2 * bit * lax.rem(lon // bit, 2))

    barrier = pltpu.get_barrier_semaphore()
    for other in [west, east] + partners[:-1]:
        pl.semaphore_signal(barrier, inc=1, device_id=(lat, other), device_id_type=MESH)

    @pl.when(has_north)
    def _():
        pl.semaphore_signal(barrier, inc=1, device_id=(lat - 1, lon), device_id_type=MESH)

    @pl.when(has_south)
    def _():
        pl.semaphore_signal(barrier, inc=1, device_id=(lat + 1, lon), device_id_type=MESH)

    keep_copy = pltpu.make_async_copy(keep_hbm, keep_ref, small_sem.at[0])
    lists_copy = pltpu.make_async_copy(lists_hbm, lists_ref, small_sem.at[1])
    keep_copy.start()
    lists_copy.start()

    def lanes(c):
        return pl.ds(pl.multiple_of(c * LANES, LANES), LANES)

    def local_copies(c):
        return (
            pltpu.make_async_copy(
                kv_hbm.at[:, :, :, lanes(c)], ext.at[c, :, HALO : HALO + TLAT, 0:COLS], loc_sem.at[c, 0]
            ),
            pltpu.make_async_copy(q_hbm.at[:, :, lanes(c)], qs.at[c], loc_sem.at[c, 1]),
        )

    def local_start(c, carry):
        for copy in local_copies(c):
            copy.start()
        return carry

    lax.fori_loop(0, NC, local_start, 0)

    def remote(src, dst, send, recv, target):
        return pltpu.make_async_remote_copy(
            src_ref=src, dst_ref=dst, send_sem=send, recv_sem=recv, device_id=target, device_id_type=MESH
        )

    def to_west(c):
        return remote(
            kv_hbm.at[:, :, 0:BLOCK, lanes(c)],
            ext.at[c, :, HALO : HALO + TLAT, COLS + BLOCK : WIDE],
            lon_send.at[c, 0], lon_recv.at[c, 0], (lat, west),
        )

    def to_east(c):
        return remote(
            kv_hbm.at[:, :, COLS - BLOCK : COLS, lanes(c)],
            ext.at[c, :, HALO : HALO + TLAT, COLS : COLS + BLOCK],
            lon_send.at[c, 1], lon_recv.at[c, 1], (lat, east),
        )

    def own_north(c):
        return remote(
            kv_hbm.at[:, :, :, lanes(c)], ext.at[c, :, HALO + TLAT : ROWS, 0:COLS],
            own_send.at[c, 0], own_recv.at[c, 0], (lat - 1, lon),
        )

    def own_south(c):
        return remote(
            kv_hbm.at[:, :, :, lanes(c)], ext.at[c, :, 0:HALO, 0:COLS],
            own_send.at[c, 1], own_recv.at[c, 1], (lat + 1, lon),
        )

    def cor_north(c):
        return remote(
            ext.at[c, :, HALO : HALO + TLAT, COLS:WIDE], ext.at[c, :, HALO + TLAT : ROWS, COLS:WIDE],
            cor_send.at[c, 0], cor_recv.at[c, 0], (lat - 1, lon),
        )

    def cor_south(c):
        return remote(
            ext.at[c, :, HALO : HALO + TLAT, COLS:WIDE], ext.at[c, :, 0:HALO, COLS:WIDE],
            cor_send.at[c, 1], cor_recv.at[c, 1], (lat + 1, lon),
        )

    def gram_copy(k, c):
        return remote(
            gsend.at[k, c], grecv.at[k, c], gs_sem.at[k, c], gr_sem.at[k, c], (lat, partners[k])
        )

    def lon_issue(c):
        to_west(c).start()
        to_east(c).start()

    def own_issue(c):
        @pl.when(has_north)
        def _():
            own_north(c).start()

        @pl.when(has_south)
        def _():
            own_south(c).start()

    pl.semaphore_wait(barrier, 1 + stages + has_north.astype(jnp.int32) + has_south.astype(jnp.int32))

    def first(c, carry):
        lon_issue(c)
        own_issue(c)
        return carry

    lax.fori_loop(0, AHEAD, first, 0)

    @pl.when(jnp.logical_not(has_north))
    def _():
        def clear(c, carry):
            ext[c, :, 0:HALO] = jnp.zeros((2, HALO, WIDE, LANES), jnp.bfloat16)
            return carry
        lax.fori_loop(0, NC, clear, 0)

    @pl.when(jnp.logical_not(has_south))
    def _():
        def clear(c, carry):
            ext[c, :, HALO + TLAT : ROWS] = jnp.zeros((2, HALO, WIDE, LANES), jnp.bfloat16)
            return carry
        lax.fori_loop(0, NC, clear, 0)

    keep_copy.wait()
    lists_copy.wait()

    block = lax.broadcasted_iota(jnp.int32, (KEYS // BLOCK, CELLS), 0)
    lane = lax.broadcasted_iota(jnp.int32, (KEYS // BLOCK, CELLS), 1)
    row = block // (WIDE // BLOCK)
    part = block - row * (WIDE // BLOCK)
    t_of = lane // COLS
    b_of = (lane - t_of * COLS) // BLOCK
    total_rows = n_lat * TLAT
    kept = jnp.zeros_like(row)
    for e in range(ROWS):
        place = lat * TLAT - HALO + e
        flag = keep_ref[jnp.clip(place, 0, total_rows - 1)]
        kept = jnp.where(row == e, flag, kept)
    place = lat * TLAT - HALO + row
    ok = (place >= 0) & (place < total_rows) & ((row == t_of + HALO) | (kept == 1))
    ok = ok & (row >= t_of) & (row <= t_of + 2 * HALO) & (part != 3 - b_of)
    step_lon = jnp.where(part < 2, part + 1 - b_of, 2 * b_of)
    cand = 3 * (row - t_of) + step_lon
    hit = jnp.zeros_like(row)
    for t in range(TLAT):
        for b in range(2):
            here = cand == lists_ref[t, b, 0]
            for j in range(1, NB):
                here = here | (cand == lists_ref[t, b, j])
            hit = jnp.where(here & (t_of == t) & (b_of == b), 1, hit)
    value = jnp.where(ok & (hit == 1), 0.0, -jnp.inf).astype(jnp.float32)
    for n in range(KEYS // BLOCK):
        bias[n] = jnp.broadcast_to(value[n : n + 1], (8, CELLS))

    ri = lax.broadcasted_iota(jnp.int32, (HD, HD), 0)
    ci = lax.broadcasted_iota(jnp.int32, (HD, HD), 1)

    def forward(c):
        to_west(c).wait_recv()
        to_east(c).wait_recv()

        @pl.when(has_north)
        def _():
            cor_north(c).start()

        @pl.when(has_south)
        def _():
            cor_south(c).start()

    def compute(c):
        for copy in local_copies(c):
            copy.wait()

        @pl.when(has_north)
        def _():
            own_south(c).wait_recv()
            cor_south(c).wait_recv()

        @pl.when(has_south)
        def _():
            own_north(c).wait_recv()
            cor_north(c).wait_recv()

        grams = []
        for g in range(GROUP):
            at = slice(g * HD, (g + 1) * HD)
            q = qs[c, :, :, at].reshape(CELLS, HD)
            k = ext[c, 0, :, :, at].reshape(KEYS, HD)
            v = ext[c, 1, :, :, at].reshape(KEYS, HD)
            s = lax.dot_general(k, q, (((1,), (1,)), ((), ())), preferred_element_type=jnp.float32)
            s = s.reshape(KEYS // BLOCK, BLOCK // 8, 8, CELLS) + bias[...][:, None]
            top = jnp.max(jnp.max(s, axis=(0, 1)), axis=0, keepdims=True)
            w = jnp.exp2((s - top) * SCALE)
            total = jnp.sum(jnp.sum(w, axis=(0, 1)), axis=0, keepdims=True)
            w = w.reshape(KEYS, CELLS).astype(jnp.bfloat16)
            mix = lax.dot_general(v, w, (((0,), (0,)), ((), ())), preferred_element_type=jnp.float32)
            mix = mix * (1.0 / total)
            a = mix.astype(jnp.bfloat16)
            out_ref[:, :, pl.ds(pl.multiple_of(c * LANES + g * HD, HD), HD)] = (
                mix.T.astype(jnp.bfloat16).reshape(TLAT, COLS, HD)
            )
            grams.append(
                lax.dot_general(a, a, (((1,), (1,)), ((), ())), preferred_element_type=jnp.float32)
            )
        g0, g1 = grams
        gsend[0, c, 0:HD] = jnp.where(ri <= ci, g0, g1).astype(jnp.bfloat16)
        diag = jnp.sum(jnp.where(ri == ci, g1, 0.0), axis=0, keepdims=True)
        gsend[0, c, HD:PACKED] = jnp.broadcast_to(diag, (PACKED - HD, HD)).astype(jnp.bfloat16)
        gram_copy(0, c).start()

    def gram_stage(k, c):
        gram_copy(k, c).wait_recv()
        both = gsend[k, c].astype(jnp.float32) + grecv[k, c].astype(jnp.float32)
        if k + 1 < stages:
            gsend[k + 1, c] = both.astype(jnp.bfloat16)
            gram_copy(k + 1, c).start()
        else:
            m = both[0:HD]
            mt = m.T
            d = jnp.broadcast_to(both[HD : HD + 1], (HD, HD))
            gram_ref[0, 2 * c] = jnp.where(ri <= ci, m, mt)
            gram_ref[0, 2 * c + 1] = jnp.where(ri > ci, m, jnp.where(ri == ci, d, mt))

    def step(s, carry):
        @pl.when(s < NC)
        def _():
            forward(s)

        @pl.when(s + AHEAD < NC)
        def _():
            lon_issue(s + AHEAD)
            own_issue(s + AHEAD)

        @pl.when((s >= 2) & (s < NC + 2))
        def _():
            compute(s - 2)

        for k in range(stages):
            @pl.when((s >= 4 + k) & (s < NC + 4 + k))
            def _():
                gram_stage(k, s - 4 - k)

        return carry

    lax.fori_loop(0, NC + 3 + stages, step, 0)

    def drain(c, carry):
        to_west(c).wait_send()
        to_east(c).wait_send()

        @pl.when(has_north)
        def _():
            own_north(c).wait_send()
            cor_north(c).wait_send()

        @pl.when(has_south)
        def _():
            own_south(c).wait_send()
            cor_south(c).wait_send()

        for k in range(stages):
            gram_copy(k, c).wait_send()
        return carry

    lax.fori_loop(0, NC, drain, 0)


def local(n_lat, n_lon, queries, keyval, keep, lists):
    stages = n_lon.bit_length() - 1
    assert n_lon == 1 << stages and queries.shape == (TLAT, COLS, HEADS * HD)
    dma = pltpu.SemaphoreType.DMA
    vmem = pl.BlockSpec(memory_space=pltpu.VMEM)
    hbm = pl.BlockSpec(memory_space=pltpu.HBM)
    return pl.pallas_call(
        functools.partial(kernel, n_lat, n_lon, stages),
        out_shape=(
            pltpu.VMEM((TLAT, COLS, HEADS * HD), jnp.bfloat16),
            pltpu.VMEM((1, HEADS, HD, HD), jnp.float32),
        ),
        in_specs=[hbm] * 4,
        out_specs=(vmem, vmem),
        scratch_shapes=[
            pltpu.SMEM(keep.shape, jnp.int32),
            pltpu.SMEM(lists.shape, jnp.int32),
            pltpu.VMEM((NC, 2, ROWS, WIDE, LANES), jnp.bfloat16),
            pltpu.VMEM((NC, TLAT, COLS, LANES), jnp.bfloat16),
            pltpu.VMEM((KEYS // BLOCK, 8, CELLS), jnp.float32),
            pltpu.VMEM((stages, NC, PACKED, HD), jnp.bfloat16),
            pltpu.VMEM((stages, NC, PACKED, HD), jnp.bfloat16),
            dma((NC, 2)), dma((NC, 2)), dma((NC, 2)), dma((NC, 2)), dma((NC, 2)), dma((NC, 2)),
            dma((stages, NC)), dma((stages, NC)), dma((NC, 2)), dma((2,)),
        ],
        compiler_params=pltpu.CompilerParams(
            collective_id=0, has_side_effects=True, vmem_limit_bytes=32 * 1024 * 1024
        ),
        cost_estimate=pl.CostEstimate(
            flops=4 * CELLS * KEYS * HEADS * HD, bytes_accessed=4 << 20, transcendentals=CELLS * KEYS * HEADS
        ),
    )(*(pltpu.with_memory_space_constraint(x, pltpu.HBM) for x in (queries, keyval, keep, lists)))


def solution(mesh):
    placed = (P("lat", "lon", None), P(None, "lat", "lon", None), P(), P("lat", "lon", None))
    return jax.shard_map(
        functools.partial(local, mesh.shape["lat"], mesh.shape["lon"]),
        mesh=mesh,
        in_specs=placed,
        out_specs=(P("lat", "lon", None), P("lat", None, None, None)),
        check_vma=False,
    )
```
